512 devices in a mesh: frame: 32 (over y_hi, x, core), space: 16 (over z, y_lo).
Axes of the slice: x: 4, y: 8 (y_hi: 4, y_lo: 2; y = y_hi * 2 + y_lo), z: 8, core: 2. Of those that a mesh axis runs over, the one named last changes fastest.
Arguments:
- current_image: float32 [64, 16, 160, 2, 160], P('frame', 'space'), may hold values from -6 to 6
- coil_maps: bfloat16 [16, 8, 160, 2, 160], P('space'), may hold values from -2 to 2
- measured_lines: float32 [64, 16, 8, 40, 2, 160], P('frame', 'space'), may hold values from -6 to 6
- sampled_lines: int32 [64, 40], P('frame'), may hold values from 0 to 159, as said below
- prior_weights: float32 [64], replicated, may hold values from 0.2 to 2
- langevin_noise: float32 [64, 16, 160, 2, 160], P('frame', 'space'), may hold values from -2 to 2
Outputs:
- next_image: float32 [64, 16, 160, 2, 160], P('frame', 'space')
The draws below stay inside these ranges and needn't reach their ends.
Inputs may be any that keep to these rules, and one draw needn't show every extreme that they name: `sampled_lines`: each frame's 40 indices are distinct and include 0 and 159, the lowest phase-encode frequencies.
All inputs are finite; a program needn't handle non-finite values.
Results may differ from the reference program's by a relative error of at most 0.005.
Values sent between devices are 32-bit elements; how exact they have to be, the bound alone decides.
A program may use at most 64 MiB of HBM per device.

```python
import math
import jax
import jax.numpy as jnp
from jax import lax

NX = 160
NY = 160
COILS = 8
LINES = 40
FRAMES = 64
SLICES = 16


def draw_sampled_lines(key, part):
    frame_keys = jax.random.split(key, FRAMES)

    def one_frame(frame_key):
        shuffled = jax.random.permutation(frame_key, NX - 2).astype(jnp.int32) + 1
        lowest = jnp.array([0, NX - 1], dtype=jnp.int32)
        return jnp.concatenate([lowest, shuffled[:LINES - 2]])
    return jax.vmap(one_frame)(frame_keys)


def steps_of(rng, dims, shards, least, largest):
    def one(position, blocks):
        heights = jax.random.uniform(jax.random.fold_in(jax.random.fold_in(rng, 6), position), (blocks,), jnp.float32, least / len(shards), largest / len(shards))
        return jnp.repeat(jnp.exp(heights), dims[position] // blocks).reshape((-1,) + (1,) * (len(dims) - position - 1))

    factor_of = one(*shards[0])
    for cut in shards[1:]:
        factor_of = factor_of * one(*cut)
    return factor_of


def bell_draw(key, dims, width, reach, pieces=(), kind=jnp.bfloat16):
    result = width * jax.random.normal(key, dims, jnp.float32)
    if pieces:
        result = result * steps_of(key, dims, pieces, -0.22, 0.18)
    return jnp.clip(result, -reach, reach).astype(kind)


def setup_inputs(seed: int = 0) -> dict:
    arg_keys = jax.random.split(jax.random.key(seed), 7)
    return {
        "current_image": bell_draw(arg_keys[0], (FRAMES, SLICES, NX, 2, NY), 1.0, 6.0, ((0, 32), (1, 16)), jnp.float32),
        "coil_maps": bell_draw(arg_keys[1], (SLICES, COILS, NX, 2, NY), 0.35, 2.0, ((0, 16),)),
        "measured_lines": bell_draw(arg_keys[2], (FRAMES, SLICES, COILS, LINES, 2, NY), 1.0, 6.0, ((0, 32), (1, 16)), jnp.float32),
        "sampled_lines": draw_sampled_lines(jax.random.fold_in(arg_keys[6], 71), 0),
        "prior_weights": jnp.clip(jnp.exp(jax.random.uniform(arg_keys[4], (FRAMES,), jnp.float32, math.log(0.2), math.log(2.0))), 0.2, 2.0),
        "langevin_noise": bell_draw(arg_keys[5], (FRAMES, SLICES, NX, 2, NY), 0.3, 2.0, ((0, 32), (1, 16)), jnp.float32),
    }


step_size = 0.5
coupling = 0.25
softness = 0.01

def cosine_pair(waves, positions, count):
    product = waves[..., None] * positions % count
    angles = 2.0 * math.pi / count * product.astype(jnp.float32)
    scale = 1.0 / math.sqrt(count)
    return (jnp.cos(angles) * scale, jnp.sin(angles) * scale)

def row_table(count):
    indices = jnp.arange(count, dtype=jnp.int32)
    cosine, sine = cosine_pair(indices, indices, count)
    upper = jnp.concatenate([cosine, -sine], axis=1)
    lower = jnp.concatenate([sine, cosine], axis=1)
    return jnp.concatenate([upper, lower], axis=0).astype(jnp.bfloat16)

def line_table(waves, count):
    positions = jnp.arange(count, dtype=jnp.int32)
    cosine, sine = cosine_pair(waves, positions, count)
    real_part = jnp.stack([cosine, sine], axis=-1)
    imag_part = jnp.stack([-sine, cosine], axis=-1)
    return jnp.stack([real_part, imag_part], axis=-4)

def sense(maps, field):
    map_re = maps[:, :, :, 0, :].astype(jnp.float32)[None]
    map_im = maps[:, :, :, 1, :].astype(jnp.float32)[None]
    field_re = field[:, :, None, :, 0, :]
    field_im = field[:, :, None, :, 1, :]
    coil_real = map_re * field_re - map_im * field_im
    coil_imag = map_re * field_im + map_im * field_re
    return jnp.stack([coil_real, coil_imag], axis=4).astype(jnp.bfloat16)

def combine(maps, back_image):
    map_re = maps[:, :, :, 0, :].astype(jnp.float32)[None]
    map_im = maps[:, :, :, 1, :].astype(jnp.float32)[None]
    back_re = back_image[:, :, :, :, 0, :]
    back_im = back_image[:, :, :, :, 1, :]
    grad_re = lax.optimization_barrier(jnp.sum(map_re * back_re + map_im * back_im, axis=2))
    grad_im = lax.optimization_barrier(jnp.sum(map_re * back_im - map_im * back_re, axis=2))
    return jnp.stack([grad_re, grad_im], axis=3)

def reference(current_image, coil_maps, measured_lines, sampled_lines, prior_weights, langevin_noise):
    rotation = row_table(NY)
    frame_tables = line_table(sampled_lines, NX).astype(jnp.bfloat16)

    def one_frame(inputs):
        field, measured, table = inputs
        coil_image = sense(coil_maps, field[None])
        shape = coil_image.shape
        flat = coil_image.reshape(shape[:4] + (2 * NY,))
        row_spectra = jnp.dot(flat, rotation, preferred_element_type=jnp.float32).astype(jnp.bfloat16).reshape(shape)
        table_wide = table.astype(jnp.float32)
        estimate = jnp.einsum('olxi,fscxiy->fscloy', table_wide, row_spectra.astype(jnp.float32))
        residual = (estimate - measured[None]).astype(jnp.bfloat16)
        back_rows = jnp.einsum('olxi,fscloy->fscxiy', table_wide, residual.astype(jnp.float32)).astype(jnp.bfloat16)
        back_image = jnp.dot(back_rows.reshape(shape[:4] + (2 * NY,)), rotation.T, preferred_element_type=jnp.float32).reshape(shape)
        return combine(coil_maps, back_image)[0]
    data_grad = lax.map(one_frame, (current_image, measured_lines, frame_tables))
    time_table = line_table(jnp.arange(FRAMES, dtype=jnp.int32), FRAMES)
    spectrum = jnp.einsum('okfi,fsxiy->ksxoy', time_table, current_image, precision=lax.Precision.HIGHEST)
    magnitude = jnp.sqrt(spectrum[:, :, :, 0, :] ** 2 + spectrum[:, :, :, 1, :] ** 2 + softness)
    shrunk = prior_weights[:, None, None, None, None] * spectrum / magnitude[:, :, :, None, :]
    prior_grad = jnp.einsum('okfi,ksxoy->fsxiy', time_table, shrunk, precision=lax.Precision.HIGHEST)
    padded = jnp.pad(current_image, ((0, 0), (1, 1), (0, 0), (0, 0), (0, 0)))
    slice_grad = coupling * (2.0 * current_image - padded[:, :-2] - padded[:, 2:])
    return current_image - step_size * (data_grad + prior_grad + slice_grad) + langevin_noise
```

```python
import math

import jax
import jax.numpy as jnp
import ml_dtypes
import numpy as np
from jax import lax
from jax.experimental import pallas as pl
from jax.experimental.pallas import tpu as pltpu
from jax.sharding import PartitionSpec as P

MESH = pl.DeviceIdType.MESH
F32, BF16 = jnp.float32, jnp.bfloat16
ROWS = COLS = 160
COILS, LINES, FRAMES = 8, 40, 64
SOFTNESS = 0.01
MAIN = 128
GROUPS = 200
PEERS = 64
HALF = 32


def dft(count):
    index = np.arange(count)
    angles = 2.0 * math.pi / count * (index[:, None] * index[None, :] % count)
    return np.cos(angles) / math.sqrt(count), -np.sin(angles) / math.sqrt(count)


def row_tables():
    real, imag = dft(COLS)
    return np.stack([real, imag]).astype(np.float32).astype(ml_dtypes.bfloat16)


def time_tables():
    real, imag = dft(FRAMES)
    upper = np.stack([real, -imag], axis=-1).reshape(FRAMES, 2 * FRAMES)
    lower = np.stack([imag, real], axis=-1).reshape(FRAMES, 2 * FRAMES)
    forward = np.concatenate([upper, lower], axis=0)
    return np.stack([forward, forward.T]).astype(np.float32)


def dot(a, b):
    return jnp.dot(a, b, preferred_element_type=F32)


def exact_dot(a, b):
    return jnp.dot(a, b, precision=lax.Precision.HIGHEST, preferred_element_type=F32)


class Place:
    def __init__(self):
        self.frame, self.space = lax.axis_index("frame"), lax.axis_index("space")
        self.base = self.space // 2 * 2
        self.z = self.space // 2
        self.lo = self.space % 2
        self.y = self.frame // 8 * 2 + self.lo
        self.x = self.frame // 2 % 4
        self.core = self.frame % 2
        self.turn = self.turn_of(self.x, self.y, self.core)
        self.slot = self.slot_of(self.y, self.frame)
        self.start = self.start_of(self.y, self.turn)

    def turn_of(self, x, y, core):
        return (x + y) % 4 * 2 + core

    def start_of(self, y, turn):
        return 25 * y + 3 * turn

    def slot_of(self, y, frame):
        return y % 2 * HALF + frame

    def frame_of(self, x, y, core):
        return y // 2 * 8 + x * 2 + core

    def device(self, y, frame):
        return (frame, self.base + y % 2)


FAR_X = (2, 1, 3, 0)


def for_peers(place, body, each_y=None):
    def one_y(y, skip_self):
        for dx in FAR_X:
            for dc in (1, 0):
                if skip_self and dx == 0 and dc == 0:
                    continue
                x, core = (place.x + dx) % 4, (place.core + dc) % 2
                body(y, place.turn_of(x, y, core), place.frame_of(x, y, core))

    @pl.loop(0, 7)
    def _(a):
        dy = (1 - a % 2) * (4 + a // 2) + a % 2 * (4 - (a + 1) // 2)
        y = (place.y + dy) % 8
        one_y(y, False)
        if each_y is not None:
            each_y(y)

    one_y(place.y, True)
    if each_y is not None:

        @pl.when(place.turn != 7)
        def _():
            each_y(place.y)


def by_turn(place, body):
    @pl.when(place.turn != 7)
    def _():
        body(3)

    @pl.when(place.turn == 7)
    def _():
        body(4)


def wait_bytes(ref, semaphore):
    pltpu.make_async_copy(ref, ref, semaphore).wait()


def kernel(
    image, maps, measured, lines, weights, noise, row_table, time_table,
    out,
    send, ret, recv, back, below, above, planes, noise_planes, raw_maps, coil_planes, lines_planes,
    line_buf, weight_buf, row_buf, time_buf, spectra, moved, total, result,
    load_sem, own_sem, fwd_send, fwd_recv, ret_send, ret_recv, z_send, z_recv,
):
    place = Place()
    loads = [
        [pltpu.make_async_copy(image.at[f, 0, :, i, :], planes.at[f, i], load_sem.at[0]) for f in range(2) for i in range(2)],
        [pltpu.make_async_copy(image.at[f, 0, :, :, pl.ds(0, MAIN)], send.at[pl.ds(0, ROWS), f], load_sem.at[1]) for f in range(2)],
        [pltpu.make_async_copy(maps.at[0], raw_maps, load_sem.at[2])],
        [
            pltpu.make_async_copy(row_table, row_buf, load_sem.at[3]),
            pltpu.make_async_copy(lines, line_buf, load_sem.at[3]),
            pltpu.make_async_copy(weights, weight_buf, load_sem.at[3]),
            pltpu.make_async_copy(time_table, time_buf, load_sem.at[3]),
        ],
        [pltpu.make_async_copy(measured.at[f, 0, :, :, i, :], lines_planes.at[f, :, i], load_sem.at[4]) for f in range(2) for i in range(2)],
        [pltpu.make_async_copy(noise.at[f, 0, :, i, :], noise_planes.at[f, i], load_sem.at[5]) for f in range(2) for i in range(2)],
    ]
    for group in loads:
        for copy in group:
            copy.start()

    def finish(which):
        for copy in loads[which]:
            copy.wait()

    barrier = pltpu.get_barrier_semaphore()

    def greet(y, turn, frame):
        pl.semaphore_signal(barrier, inc=1, device_id=place.device(y, frame), device_id_type=MESH)

    for_peers(place, greet)

    @pl.when(place.z < 7)
    def _():
        pl.semaphore_signal(barrier, inc=1, device_id=(place.frame, place.space + 2), device_id_type=MESH)

    @pl.when(place.z > 0)
    def _():
        pl.semaphore_signal(barrier, inc=1, device_id=(place.frame, place.space - 2), device_id_type=MESH)

    finish(0)
    finish(1)
    for f in range(2):
        for i in range(2):
            tails = [planes[f, i, 40 * b : 40 * b + 40, MAIN:COLS] for b in range(4)]
            send[pl.ds(ROWS, 40), f, i, :] = jnp.concatenate(tails, axis=1)

    finish(2)

    @pl.loop(0, COILS)
    def _(c):
        for i in range(2):
            coil_planes[c, i] = raw_maps[c, :, i, :].astype(F32)

    @pl.when((place.z == 0) | (place.z == 7))
    def _():
        pl.semaphore_wait(barrier, PEERS)

    @pl.when((place.z != 0) & (place.z != 7))
    def _():
        pl.semaphore_wait(barrier, PEERS + 1)

    def send_fwd(y, turn, frame):
        pltpu.make_async_remote_copy(
            send.at[pl.ds(place.start_of(y, turn), 3)],
            recv.at[pl.ds(0, 3), place.slot],
            fwd_send, fwd_recv, device_id=place.device(y, frame), device_id_type=MESH,
        ).start()

    def send_extra(y):
        frame = place.frame_of((7 - y) % 4, y, 1)
        pltpu.make_async_remote_copy(
            send.at[pl.ds(25 * y + 24, 1)],
            recv.at[pl.ds(3, 1), place.slot],
            fwd_send, fwd_recv, device_id=place.device(y, frame), device_id_type=MESH,
        ).start()

    for_peers(place, send_fwd, send_extra)

    def keep_own(count):
        copy = pltpu.make_async_copy(send.at[pl.ds(place.start, count)], recv.at[pl.ds(0, count), place.slot], own_sem)
        copy.start()
        copy.wait()

    by_turn(place, keep_own)

    finish(3)
    finish(4)
    real, imag = row_buf[0], row_buf[1]
    positions = lax.broadcasted_iota(jnp.int32, (COLS, LINES), 0)

    @pl.loop(0, 2)
    def _(f):
        chosen = (positions == line_buf[pl.ds(f, 1), :]).astype(F32).astype(BF16)
        pick = (((0,), (0,)), ((), ()))
        line_real = lax.dot_general(chosen, real, pick, preferred_element_type=F32)
        line_imag = lax.dot_general(chosen, imag, pick, preferred_element_type=F32)
        table = jnp.concatenate([line_real, line_imag], axis=0)
        turned = jnp.concatenate([-line_imag, line_real], axis=0)
        back_table = jnp.concatenate([table.T, turned.T], axis=0).astype(BF16)
        table = table.astype(BF16)
        x_re, x_im = planes[f, 0], planes[f, 1]

        @pl.loop(0, COILS, unroll=2)
        def _(c):
            s_re, s_im = coil_planes[c, 0], coil_planes[c, 1]
            c_re = (s_re * x_re - s_im * x_im).astype(BF16)
            c_im = (s_re * x_im + s_im * x_re).astype(BF16)
            first, second = dot(table, c_re), dot(table, c_im)
            spectra[c, 0:LINES] = first[:LINES] - second[LINES:]
            spectra[c, LINES:] = first[LINES:] + second[:LINES]

        @pl.loop(0, COILS, unroll=2)
        def _(c):
            rows = spectra[c].astype(BF16)
            first, second = dot(rows, real), dot(rows, imag)
            res_re = first[:LINES] - second[LINES:] - lines_planes[f, c, 0]
            res_im = first[LINES:] + second[:LINES] - lines_planes[f, c, 1]
            residual = jnp.concatenate([res_re, res_im], axis=0).astype(BF16)
            first, second = dot(residual, real), dot(residual, imag)
            moved[c, 0:LINES] = first[:LINES] + second[LINES:]
            moved[c, LINES:] = first[LINES:] - second[:LINES]

        total[...] = jnp.zeros_like(total)

        @pl.loop(0, COILS, unroll=2)
        def _(c):
            full = dot(back_table, moved[c].astype(BF16))
            s_re, s_im = coil_planes[c, 0], coil_planes[c, 1]
            b_re, b_im = full[:ROWS], full[ROWS:]
            total[0] += s_re * b_re + s_im * b_im
            total[1] += s_re * b_im - s_im * b_re

        for i in range(2):
            result[f, i] = 0.75 * planes[f, i] - 0.5 * total[i]

    finish(5)
    for f in range(2):
        for i in range(2):
            result[f, i] += noise_planes[f, i]

    spot = (lax.broadcasted_iota(jnp.int32, (FRAMES, FRAMES), 0) == lax.broadcasted_iota(jnp.int32, (FRAMES, FRAMES), 1))
    column = -0.5 * jnp.sum(jnp.where(spot, weight_buf[...], 0.0), axis=1, keepdims=True)

    def up_copy(count):
        return pltpu.make_async_remote_copy(
            recv.at[pl.ds(0, count), pl.ds(HALF, HALF)], below.at[pl.ds(0, count)],
            z_send.at[0], z_recv.at[0], device_id=(place.frame, place.space + 2), device_id_type=MESH,
        )

    def down_copy(count):
        return pltpu.make_async_remote_copy(
            recv.at[pl.ds(0, count), pl.ds(0, HALF)], above.at[pl.ds(0, count)],
            z_send.at[1], z_recv.at[1], device_id=(place.frame, place.space - 2), device_id_type=MESH,
        )

    def prior(count):
        wait_bytes(recv.at[pl.ds(0, count), pl.ds(0, PEERS - 1)], fwd_recv)

        @pl.when(place.z < 7)
        def _():
            up_copy(count).start()

        @pl.when(place.z > 0)
        def _():
            down_copy(count).start()

        rows_in, rows_out = recv.reshape(4 * 4 * PEERS, MAIN), back.reshape(4 * 4 * PEERS, MAIN)
        rows_below, rows_above = below.reshape(4 * 4 * HALF, MAIN), above.reshape(4 * 4 * HALF, MAIN)

        def span(first, g):
            return pl.ds(4 * (PEERS * g + first), 4 * HALF)

        blocks = [(first, g) for first in (0, HALF) for g in range(count)]
        stack = jnp.concatenate([rows_in[span(first, g), :] for first, g in blocks], axis=1)
        spectrum = exact_dot(time_buf[0], stack)
        s_re, s_im = spectrum[:FRAMES], spectrum[FRAMES:]
        scale = column * lax.rsqrt(s_re * s_re + s_im * s_im + SOFTNESS)
        shrunk = jnp.concatenate([s_re * scale, s_im * scale], axis=0)
        gradient = exact_dot(time_buf[1], shrunk)
        for n, (first, g) in enumerate(blocks):
            beside = rows_in[span(HALF - first, g), :]
            rows_out[span(first, g), :] = gradient[:, n * MAIN : (n + 1) * MAIN] + 0.125 * beside

        @pl.when(place.z > 0)
        def _():
            up_copy(count).wait_recv()
            for g in range(count):
                rows_out[span(0, g), :] += 0.125 * rows_below[pl.ds(4 * HALF * g, 4 * HALF), :]

        @pl.when(place.z < 7)
        def _():
            down_copy(count).wait_recv()
            for g in range(count):
                rows_out[span(HALF, g), :] += 0.125 * rows_above[pl.ds(4 * HALF * g, 4 * HALF), :]

        def send_back(y, turn, frame):
            pltpu.make_async_remote_copy(
                back.at[pl.ds(0, count), place.slot_of(y, frame)],
                ret.at[pl.ds(place.start, count)],
                ret_send, ret_recv, device_id=place.device(y, frame), device_id_type=MESH,
            ).start()

        for_peers(place, send_back)
        copy = pltpu.make_async_copy(back.at[pl.ds(0, count), place.slot], ret.at[pl.ds(place.start, count)], own_sem)
        copy.start()
        copy.wait()
        wait_bytes(ret.at[pl.ds(0, GROUPS - count)], ret_recv)

    by_turn(place, prior)

    for f in range(2):
        for i in range(2):
            out[f, 0, :, i, 0:MAIN] = result[f, i, :, 0:MAIN] + ret[pl.ds(0, ROWS), f, i, :]
            tails = ret[pl.ds(ROWS, 40), f, i, :]
            tails = jnp.concatenate([tails[:, 32 * b : 32 * b + 32] for b in range(4)], axis=0)
            out[f, 0, :, i, MAIN:COLS] = result[f, i, :, MAIN:COLS] + tails

    def drain(count):
        wait_bytes(send.at[pl.ds(0, GROUPS - count)], fwd_send)
        wait_bytes(recv.at[pl.ds(0, count), pl.ds(0, PEERS - 1)], ret_send)

        @pl.when(place.z < 7)
        def _():
            up_copy(count).wait_send()

        @pl.when(place.z > 0)
        def _():
            down_copy(count).wait_send()

    by_turn(place, drain)


def on_device(image, maps, measured, lines, weights, noise):
    dma = pltpu.SemaphoreType.DMA
    anywhere = pl.BlockSpec(memory_space=pl.ANY)
    return pl.pallas_call(
        kernel,
        name="langevin_step",
        out_shape=jax.ShapeDtypeStruct(image.shape, F32),
        in_specs=[anywhere] * 8,
        out_specs=pl.BlockSpec(memory_space=pltpu.VMEM),
        scratch_shapes=[
            pltpu.VMEM((GROUPS, 2, 2, MAIN), F32),
            pltpu.VMEM((GROUPS, 2, 2, MAIN), F32),
            pltpu.VMEM((4, PEERS, 2, 2, MAIN), F32),
            pltpu.VMEM((4, PEERS, 2, 2, MAIN), F32),
            pltpu.VMEM((4, HALF, 2, 2, MAIN), F32),
            pltpu.VMEM((4, HALF, 2, 2, MAIN), F32),
            pltpu.VMEM((2, 2, ROWS, COLS), F32),
            pltpu.VMEM((2, 2, ROWS, COLS), F32),
            pltpu.VMEM((COILS, ROWS, 2, COLS), BF16),
            pltpu.VMEM((COILS, 2, ROWS, COLS), F32),
            pltpu.VMEM((2, COILS, 2, LINES, COLS), F32),
            pltpu.VMEM((2, LINES), jnp.int32),
            pltpu.VMEM((1, FRAMES), F32),
            pltpu.VMEM((2, COLS, COLS), BF16),
            pltpu.VMEM((2, 2 * FRAMES, 2 * FRAMES), F32),
            pltpu.VMEM((COILS, 2 * LINES, COLS), F32),
            pltpu.VMEM((COILS, 2 * LINES, COLS), F32),
            pltpu.VMEM((2, ROWS, COLS), F32),
            pltpu.VMEM((2, 2, ROWS, COLS), F32),
            dma((6,)), dma, dma, dma, dma, dma, dma((2,)), dma((2,)),
        ],
        compiler_params=pltpu.CompilerParams(collective_id=0, has_side_effects=True, vmem_limit_bytes=40 << 20),
        cost_estimate=pl.CostEstimate(flops=2_000_000_000, bytes_accessed=6_000_000, transcendentals=60_000),
    )(image, maps, measured, lines, weights.reshape(1, FRAMES), noise, jnp.asarray(row_tables()), jnp.asarray(time_tables()))


def solution(mesh):
    return jax.shard_map(
        on_device,
        mesh=mesh,
        in_specs=(
            P("frame", "space", None, None, None),
            P("space", None, None, None, None),
            P("frame", "space", None, None, None, None),
            P("frame", None),
            P(),
            P("frame", "space", None, None, None),
        ),
        out_specs=P("frame", "space", None, None, None),
        check_vma=False,
    )
```

```python
import math

import jax
import jax.numpy as jnp
import ml_dtypes
import numpy as np
from jax import lax
from jax.experimental import pallas as pl
from jax.experimental.pallas import tpu as pltpu
from jax.sharding import PartitionSpec as P

MESH = pl.DeviceIdType.MESH
F32, BF16 = jnp.float32, jnp.bfloat16
ROWS = COLS = 160
COILS, LINES, FRAMES = 8, 40, 64
SOFTNESS = 0.01
MAIN = 128
GROUPS = 200
PEERS = 64
HALF = 32


def dft(count):
    index = np.arange(count)
    angles = 2.0 * math.pi / count * (index[:, None] * index[None, :] % count)
    return np.cos(angles) / math.sqrt(count), -np.sin(angles) / math.sqrt(count)


def row_tables():
    real, imag = dft(COLS)
    return np.stack([real, imag]).astype(np.float32).astype(ml_dtypes.bfloat16)


def time_tables():
    real, imag = dft(FRAMES)
    upper = np.stack([real, -imag], axis=-1).reshape(FRAMES, 2 * FRAMES)
    lower = np.stack([imag, real], axis=-1).reshape(FRAMES, 2 * FRAMES)
    forward = np.concatenate([upper, lower], axis=0)
    return np.stack([forward, forward.T]).astype(np.float32)


def dot(a, b):
    return jnp.dot(a, b, preferred_element_type=F32)


def exact_dot(a, b):
    return jnp.dot(a, b, precision=lax.Precision.HIGHEST, preferred_element_type=F32)


class Place:
    def __init__(self):
        self.frame, self.space = lax.axis_index("frame"), lax.axis_index("space")
        self.base = self.space // 2 * 2
        self.z = self.space // 2
        self.lo = self.space % 2
        self.y = self.frame // 8 * 2 + self.lo
        self.x = self.frame // 2 % 4
        self.core = self.frame % 2
        self.turn = self.turn_of(self.x, self.y, self.core)
        self.slot = self.slot_of(self.y, self.frame)
        self.start = self.start_of(self.y, self.turn)

    def turn_of(self, x, y, core):
        return (x + y) % 4 * 2 + core

    def start_of(self, y, turn):
        return 25 * y + 3 * turn

    def slot_of(self, y, frame):
        return y % 2 * HALF + frame

    def frame_of(self, x, y, core):
        return y // 2 * 8 + x * 2 + core

    def device(self, y, frame):
        return (frame, self.base + y % 2)


FAR_X = (2, 1, 3, 0)


def for_peers(place, body, each_y=None):
    def one_y(y, skip_self):
        for dx in FAR_X:
            for dc in (1, 0):
                if skip_self and dx == 0 and dc == 0:
                    continue
                x, core = (place.x + dx) % 4, (place.core + dc) % 2
                body(y, place.turn_of(x, y, core), place.frame_of(x, y, core))

    @pl.loop(0, 7)
    def _(a):
        dy = (1 - a % 2) * (4 + a // 2) + a % 2 * (4 - (a + 1) // 2)
        y = (place.y + dy) % 8
        one_y(y, False)
        if each_y is not None:
            each_y(y)

    one_y(place.y, True)
    if each_y is not None:

        @pl.when(place.turn != 7)
        def _():
            each_y(place.y)


def by_turn(place, body):
    @pl.when(place.turn != 7)
    def _():
        body(3)

    @pl.when(place.turn == 7)
    def _():
        body(4)


def wait_bytes(ref, semaphore):
    pltpu.make_async_copy(ref, ref, semaphore).wait()


def kernel(
    image, maps, measured, lines, weights, noise, row_table, time_table,
    out,
    send, ret, recv, back, below, above, planes, noise_planes, raw_maps, coil_planes, lines_planes,
    line_buf, weight_buf, row_buf, time_buf, back_table, spectra, moved, total, result,
    load_sem, own_sem, fwd_send, fwd_recv, ret_send, ret_recv, z_send, z_recv,
):
    place = Place()
    loads = [
        [pltpu.make_async_copy(image.at[f, 0, :, i, :], planes.at[f, i], load_sem.at[0]) for f in range(2) for i in range(2)],
        [pltpu.make_async_copy(image.at[f, 0, :, :, pl.ds(0, MAIN)], send.at[pl.ds(0, ROWS), f], load_sem.at[1]) for f in range(2)],
        [pltpu.make_async_copy(maps.at[0], raw_maps, load_sem.at[2])],
        [
            pltpu.make_async_copy(row_table, row_buf, load_sem.at[3]),
            pltpu.make_async_copy(lines, line_buf, load_sem.at[3]),
            pltpu.make_async_copy(weights, weight_buf, load_sem.at[3]),
            pltpu.make_async_copy(time_table, time_buf, load_sem.at[3]),
        ],
        [pltpu.make_async_copy(measured.at[f, 0, :, :, i, :], lines_planes.at[f, :, i], load_sem.at[4]) for f in range(2) for i in range(2)],
        [pltpu.make_async_copy(noise.at[f, 0, :, i, :], noise_planes.at[f, i], load_sem.at[5]) for f in range(2) for i in range(2)],
    ]
    for group in loads:
        for copy in group:
            copy.start()

    def finish(which):
        for copy in loads[which]:
            copy.wait()

    barrier = pltpu.get_barrier_semaphore()

    def greet(y, turn, frame):
        pl.semaphore_signal(barrier, inc=1, device_id=place.device(y, frame), device_id_type=MESH)

    for_peers(place, greet)

    @pl.when(place.z < 7)
    def _():
        pl.semaphore_signal(barrier, inc=1, device_id=(place.frame, place.space + 2), device_id_type=MESH)

    @pl.when(place.z > 0)
    def _():
        pl.semaphore_signal(barrier, inc=1, device_id=(place.frame, place.space - 2), device_id_type=MESH)

    finish(0)
    finish(1)
    for f in range(2):
        for i in range(2):
            tails = [planes[f, i, 40 * b : 40 * b + 40, MAIN:COLS] for b in range(4)]
            send[pl.ds(ROWS, 40), f, i, :] = jnp.concatenate(tails, axis=1)

    finish(2)

    @pl.loop(0, COILS)
    def _(c):
        for i in range(2):
            coil_planes[c, i] = raw_maps[c, :, i, :].astype(F32)

    @pl.when((place.z == 0) | (place.z == 7))
    def _():
        pl.semaphore_wait(barrier, PEERS)

    @pl.when((place.z != 0) & (place.z != 7))
    def _():
        pl.semaphore_wait(barrier, PEERS + 1)

    for k in range(3):

        def send_fwd(y, turn, frame):
            pltpu.make_async_remote_copy(
                send.at[pl.ds(place.start_of(y, turn) + k, 1)],
                recv.at[pl.ds(k, 1), place.slot],
                fwd_send, fwd_recv.at[k], device_id=place.device(y, frame), device_id_type=MESH,
            ).start()

        def send_extra(y):
            frame = place.frame_of((7 - y) % 4, y, 1)
            pltpu.make_async_remote_copy(
                send.at[pl.ds(25 * y + 24, 1)],
                recv.at[pl.ds(3, 1), place.slot],
                fwd_send, fwd_recv.at[2], device_id=place.device(y, frame), device_id_type=MESH,
            ).start()

        for_peers(place, send_fwd, send_extra if k == 2 else None)

    def keep_own(count):
        copy = pltpu.make_async_copy(send.at[pl.ds(place.start, count)], recv.at[pl.ds(0, count), place.slot], own_sem)
        copy.start()
        copy.wait()

    by_turn(place, keep_own)

    finish(3)
    finish(4)
    finish(5)
    real, imag = row_buf[0], row_buf[1]
    positions = lax.broadcasted_iota(jnp.int32, (COLS, LINES), 0)

    def to_lines(f):
        chosen = (positions == line_buf[pl.ds(f, 1), :]).astype(F32).astype(BF16)
        pick = (((0,), (0,)), ((), ()))
        line_real = lax.dot_general(chosen, real, pick, preferred_element_type=F32)
        line_imag = lax.dot_general(chosen, imag, pick, preferred_element_type=F32)
        table = jnp.concatenate([line_real, line_imag], axis=0)
        turned = jnp.concatenate([-line_imag, line_real], axis=0)
        back_table[...] = jnp.concatenate([table.T, turned.T], axis=0).astype(BF16)
        table = table.astype(BF16)
        x_re, x_im = planes[f, 0], planes[f, 1]

        @pl.loop(0, COILS, unroll=2)
        def _(c):
            s_re, s_im = coil_planes[c, 0], coil_planes[c, 1]
            c_re = (s_re * x_re - s_im * x_im).astype(BF16)
            c_im = (s_re * x_im + s_im * x_re).astype(BF16)
            first, second = dot(table, c_re), dot(table, c_im)
            spectra[c, 0:LINES] = first[:LINES] - second[LINES:]
            spectra[c, LINES:] = first[LINES:] + second[:LINES]

    def to_residual(f):
        @pl.loop(0, COILS, unroll=2)
        def _(c):
            rows = spectra[c].astype(BF16)
            first, second = dot(rows, real), dot(rows, imag)
            res_re = first[:LINES] - second[LINES:] - lines_planes[f, c, 0]
            res_im = first[LINES:] + second[:LINES] - lines_planes[f, c, 1]
            residual = jnp.concatenate([res_re, res_im], axis=0).astype(BF16)
            first, second = dot(residual, real), dot(residual, imag)
            moved[c, 0:LINES] = first[:LINES] + second[LINES:]
            moved[c, LINES:] = first[LINES:] - second[:LINES]

    def to_image(f):
        total[...] = jnp.zeros_like(total)

        @pl.loop(0, COILS, unroll=2)
        def _(c):
            full = dot(back_table[...], moved[c].astype(BF16))
            s_re, s_im = coil_planes[c, 0], coil_planes[c, 1]
            b_re, b_im = full[:ROWS], full[ROWS:]
            total[0] += s_re * b_re + s_im * b_im
            total[1] += s_re * b_im - s_im * b_re

        for i in range(2):
            result[f, i] = 0.75 * planes[f, i] - 0.5 * total[i] + noise_planes[f, i]

    spot = (lax.broadcasted_iota(jnp.int32, (FRAMES, FRAMES), 0) == lax.broadcasted_iota(jnp.int32, (FRAMES, FRAMES), 1))
    column = -0.5 * jnp.sum(jnp.where(spot, weight_buf[...], 0.0), axis=1, keepdims=True)

    def up_copy(k, count):
        return pltpu.make_async_remote_copy(
            recv.at[pl.ds(k, count), pl.ds(HALF, HALF)], below.at[pl.ds(k, count)],
            z_send.at[k, 0], z_recv.at[k, 0], device_id=(place.frame, place.space + 2), device_id_type=MESH,
        )

    def down_copy(k, count):
        return pltpu.make_async_remote_copy(
            recv.at[pl.ds(k, count), pl.ds(0, HALF)], above.at[pl.ds(k, count)],
            z_send.at[k, 1], z_recv.at[k, 1], device_id=(place.frame, place.space - 2), device_id_type=MESH,
        )

    rows_in, rows_out = recv.reshape(4 * 4 * PEERS, MAIN), back.reshape(4 * 4 * PEERS, MAIN)
    rows_below, rows_above = below.reshape(4 * 4 * HALF, MAIN), above.reshape(4 * 4 * HALF, MAIN)

    def span(first, g):
        return pl.ds(4 * (PEERS * g + first), 4 * HALF)

    def arrive(k, count):
        wait_bytes(recv.at[pl.ds(k, count), pl.ds(0, PEERS - 1)], fwd_recv.at[k])

        @pl.when(place.z < 7)
        def _():
            up_copy(k, count).start()

        @pl.when(place.z > 0)
        def _():
            down_copy(k, count).start()

        blocks = [(first, g) for first in (0, HALF) for g in range(k, k + count)]
        stack = jnp.concatenate([rows_in[span(first, g), :] for first, g in blocks], axis=1)
        spectrum = exact_dot(time_buf[0], stack)
        s_re, s_im = spectrum[:FRAMES], spectrum[FRAMES:]
        scale = column * lax.rsqrt(s_re * s_re + s_im * s_im + SOFTNESS)
        shrunk = jnp.concatenate([s_re * scale, s_im * scale], axis=0)
        gradient = exact_dot(time_buf[1], shrunk)
        for n, (first, g) in enumerate(blocks):
            beside = rows_in[span(HALF - first, g), :]
            rows_out[span(first, g), :] = gradient[:, n * MAIN : (n + 1) * MAIN] + 0.125 * beside

    def leave(k, count):
        @pl.when(place.z > 0)
        def _():
            up_copy(k, count).wait_recv()
            for g in range(k, k + count):
                rows_out[span(0, g), :] += 0.125 * rows_below[pl.ds(4 * HALF * g, 4 * HALF), :]

        @pl.when(place.z < 7)
        def _():
            down_copy(k, count).wait_recv()
            for g in range(k, k + count):
                rows_out[span(HALF, g), :] += 0.125 * rows_above[pl.ds(4 * HALF * g, 4 * HALF), :]

        def send_back(y, turn, frame):
            pltpu.make_async_remote_copy(
                back.at[pl.ds(k, count), place.slot_of(y, frame)],
                ret.at[pl.ds(place.start + k, count)],
                ret_send, ret_recv, device_id=place.device(y, frame), device_id_type=MESH,
            ).start()

        for_peers(place, send_back)

    to_lines(0)
    arrive(0, 1)
    to_residual(0)
    arrive(1, 1)
    leave(0, 1)
    by_turn(place, lambda count: arrive(2, count - 2))
    leave(1, 1)
    to_image(0)
    by_turn(place, lambda count: leave(2, count - 2))
    to_lines(1)
    to_residual(1)
    to_image(1)

    def settle(count):
        copy = pltpu.make_async_copy(back.at[pl.ds(0, count), place.slot], ret.at[pl.ds(place.start, count)], own_sem)
        copy.start()
        copy.wait()
        wait_bytes(ret.at[pl.ds(0, GROUPS - count)], ret_recv)

    by_turn(place, settle)

    for f in range(2):
        for i in range(2):
            out[f, 0, :, i, 0:MAIN] = result[f, i, :, 0:MAIN] + ret[pl.ds(0, ROWS), f, i, :]
            tails = ret[pl.ds(ROWS, 40), f, i, :]
            tails = jnp.concatenate([tails[:, 32 * b : 32 * b + 32] for b in range(4)], axis=0)
            out[f, 0, :, i, MAIN:COLS] = result[f, i, :, MAIN:COLS] + tails

    def drain(count):
        wait_bytes(send.at[pl.ds(0, GROUPS - count)], fwd_send)
        wait_bytes(recv.at[pl.ds(0, count), pl.ds(0, PEERS - 1)], ret_send)

        for k in range(3):
            groups = count - 2 if k == 2 else 1

            @pl.when(place.z < 7)
            def _():
                up_copy(k, groups).wait_send()

            @pl.when(place.z > 0)
            def _():
                down_copy(k, groups).wait_send()

    by_turn(place, drain)


def on_device(image, maps, measured, lines, weights, noise):
    dma = pltpu.SemaphoreType.DMA
    anywhere = pl.BlockSpec(memory_space=pl.ANY)
    return pl.pallas_call(
        kernel,
        name="langevin_step",
        out_shape=jax.ShapeDtypeStruct(image.shape, F32),
        in_specs=[anywhere] * 8,
        out_specs=pl.BlockSpec(memory_space=pltpu.VMEM),
        scratch_shapes=[
            pltpu.VMEM((GROUPS, 2, 2, MAIN), F32),
            pltpu.VMEM((GROUPS, 2, 2, MAIN), F32),
            pltpu.VMEM((4, PEERS, 2, 2, MAIN), F32),
            pltpu.VMEM((4, PEERS, 2, 2, MAIN), F32),
            pltpu.VMEM((4, HALF, 2, 2, MAIN), F32),
            pltpu.VMEM((4, HALF, 2, 2, MAIN), F32),
            pltpu.VMEM((2, 2, ROWS, COLS), F32),
            pltpu.VMEM((2, 2, ROWS, COLS), F32),
            pltpu.VMEM((COILS, ROWS, 2, COLS), BF16),
            pltpu.VMEM((COILS, 2, ROWS, COLS), F32),
            pltpu.VMEM((2, COILS, 2, LINES, COLS), F32),
            pltpu.VMEM((2, LINES), jnp.int32),
            pltpu.VMEM((1, FRAMES), F32),
            pltpu.VMEM((2, COLS, COLS), BF16),
            pltpu.VMEM((2, 2 * FRAMES, 2 * FRAMES), F32),
            pltpu.VMEM((2 * ROWS, 2 * LINES), BF16),
            pltpu.VMEM((COILS, 2 * LINES, COLS), F32),
            pltpu.VMEM((COILS, 2 * LINES, COLS), F32),
            pltpu.VMEM((2, ROWS, COLS), F32),
            pltpu.VMEM((2, 2, ROWS, COLS), F32),
            dma((6,)), dma, dma, dma((3,)), dma, dma, dma((3, 2)), dma((3, 2)),
        ],
        compiler_params=pltpu.CompilerParams(collective_id=0, has_side_effects=True, vmem_limit_bytes=60 << 20),
        cost_estimate=pl.CostEstimate(flops=2_000_000_000, bytes_accessed=6_000_000, transcendentals=60_000),
    )(image, maps, measured, lines, weights.reshape(1, FRAMES), noise, jnp.asarray(row_tables()), jnp.asarray(time_tables()))


def solution(mesh):
    return jax.shard_map(
        on_device,
        mesh=mesh,
        in_specs=(
            P("frame", "space", None, None, None),
            P("space", None, None, None, None),
            P("frame", "space", None, None, None, None),
            P("frame", None),
            P(),
            P("frame", "space", None, None, None),
        ),
        out_specs=P("frame", "space", None, None, None),
        check_vma=False,
    )
```

```python
import math

import jax
import jax.numpy as jnp
import ml_dtypes
import numpy as np
from jax import lax
from jax.experimental import pallas as pl
from jax.experimental.pallas import tpu as pltpu
from jax.sharding import PartitionSpec as P

MESH = pl.DeviceIdType.MESH
F32, BF16 = jnp.float32, jnp.bfloat16
ROWS = COLS = 160
COILS, LINES, FRAMES = 8, 40, 64
SOFTNESS = 0.01
MAIN = 128
GROUPS = 200
PEERS = 64
HALF = 32


def dft(count):
    index = np.arange(count)
    angles = 2.0 * math.pi / count * (index[:, None] * index[None, :] % count)
    return np.cos(angles) / math.sqrt(count), -np.sin(angles) / math.sqrt(count)


def row_tables():
    real, imag = dft(COLS)
    return np.stack([real, imag]).astype(np.float32).astype(ml_dtypes.bfloat16)


def time_tables():
    real, imag = dft(FRAMES)
    upper = np.stack([real, -imag], axis=-1).reshape(FRAMES, 2 * FRAMES)
    lower = np.stack([imag, real], axis=-1).reshape(FRAMES, 2 * FRAMES)
    forward = np.concatenate([upper, lower], axis=0)
    return np.stack([forward, forward.T]).astype(np.float32)


def dot(a, b):
    return jnp.dot(a, b, preferred_element_type=F32)


def exact_dot(a, b):
    return jnp.dot(a, b, precision=lax.Precision.HIGHEST, preferred_element_type=F32)


class Place:
    def __init__(self):
        self.frame, self.space = lax.axis_index("frame"), lax.axis_index("space")
        self.base = self.space // 2 * 2
        self.z = self.space // 2
        self.y = self.frame // 8 * 2 + self.space % 2
        x, core = self.frame // 2 % 4, self.frame % 2
        self.xs = [(x + dx) % 4 for dx in FAR_X]
        self.cores = [1 - core, core]
        self.turn = (x + self.y) % 4 * 2 + core
        self.slot = self.space % 2 * HALF + self.frame
        self.start = 25 * self.y + 3 * self.turn


class Peer:
    def __init__(self, frame, space, slot, start):
        self.device, self.slot, self.start = (frame, space), slot, start


FAR_X = (2, 1, 3, 0)


def row_of(place, y):
    frame, space, slot, start = y // 2 * 8, place.base + y % 2, y % 2 * HALF + y // 2 * 8, 25 * y
    peers = []
    for x in place.xs:
        first = start + 6 * ((x + y) % 4)
        for core in place.cores:
            at = 2 * x + core
            peers.append(Peer(frame + at, space, slot + at, first + 3 * core))
    extra = (7 - y) % 4 * 2 + 1
    return peers, Peer(frame + extra, space, slot + extra, start + 21)


def for_peers(place, body, each_row=None):
    @pl.loop(0, 7)
    def _(a):
        dy = (1 - a % 2) * (4 + a // 2) + a % 2 * (4 - (a + 1) // 2)
        peers, extra = row_of(place, (place.y + dy) % 8)
        for peer in peers:
            body(peer)
        if each_row is not None:
            each_row(extra)

    peers, extra = row_of(place, place.y)
    for peer in peers[:-1]:
        body(peer)
    if each_row is not None:

        @pl.when(place.turn != 7)
        def _():
            each_row(extra)


def by_turn(place, body):
    @pl.when(place.turn != 7)
    def _():
        body(3)

    @pl.when(place.turn == 7)
    def _():
        body(4)


def wait_bytes(ref, semaphore):
    pltpu.make_async_copy(ref, ref, semaphore).wait()


def kernel(
    image, maps, measured, lines, weights, noise, row_table, time_table,
    ret, known,
    send, recv, back, below, above, planes, noise_planes, raw_maps, coil_planes, lines_planes,
    line_buf, weight_buf, row_buf, time_buf, back_table, spectra, moved, total, result,
    load_sem, own_sem, fwd_send, fwd_recv, ret_send, ret_recv, z_send, z_recv,
):
    place = Place()
    loads = [
        [pltpu.make_async_copy(image.at[f, 0, :, i, :], planes.at[f, i], load_sem.at[0]) for f in range(2) for i in range(2)],
        [pltpu.make_async_copy(image.at[f, 0, :, :, pl.ds(0, MAIN)], send.at[pl.ds(0, ROWS), f], load_sem.at[1]) for f in range(2)],
        [pltpu.make_async_copy(maps.at[0], raw_maps, load_sem.at[2])],
        [
            pltpu.make_async_copy(row_table, row_buf, load_sem.at[3]),
            pltpu.make_async_copy(lines, line_buf, load_sem.at[3]),
            pltpu.make_async_copy(weights, weight_buf, load_sem.at[3]),
            pltpu.make_async_copy(time_table, time_buf, load_sem.at[3]),
        ],
        [pltpu.make_async_copy(measured.at[f, 0, :, :, i, :], lines_planes.at[f, :, i], load_sem.at[4]) for f in range(2) for i in range(2)],
        [pltpu.make_async_copy(noise.at[f, 0, :, i, :], noise_planes.at[f, i], load_sem.at[5]) for f in range(2) for i in range(2)],
    ]
    for copy in loads[1] + loads[0]:
        copy.start()

    def finish(which):
        for copy in loads[which]:
            copy.wait()

    barrier = pltpu.get_barrier_semaphore()

    def greet(peer):
        pl.semaphore_signal(barrier, inc=1, device_id=peer.device, device_id_type=MESH)

    for_peers(place, greet)
    for group in loads[2:]:
        for copy in group:
            copy.start()

    @pl.when(place.z < 7)
    def _():
        pl.semaphore_signal(barrier, inc=1, device_id=(place.frame, place.space + 2), device_id_type=MESH)

    @pl.when(place.z > 0)
    def _():
        pl.semaphore_signal(barrier, inc=1, device_id=(place.frame, place.space - 2), device_id_type=MESH)

    finish(0)
    finish(1)
    for f in range(2):
        for i in range(2):
            tails = [planes[f, i, 40 * b : 40 * b + 40, MAIN:COLS] for b in range(4)]
            send[pl.ds(ROWS, 40), f, i, :] = jnp.concatenate(tails, axis=1)

    finish(2)

    @pl.loop(0, COILS)
    def _(c):
        for i in range(2):
            coil_planes[c, i] = raw_maps[c, :, i, :].astype(F32)

    @pl.when((place.z == 0) | (place.z == 7))
    def _():
        pl.semaphore_wait(barrier, PEERS)

    @pl.when((place.z != 0) & (place.z != 7))
    def _():
        pl.semaphore_wait(barrier, PEERS + 1)

    for k in range(3):

        def send_fwd(peer):
            pltpu.make_async_remote_copy(
                send.at[pl.ds(peer.start + k, 1)],
                recv.at[pl.ds(k, 1), place.slot],
                fwd_send, fwd_recv.at[k], device_id=peer.device, device_id_type=MESH,
            ).start()

        def send_extra(peer):
            pltpu.make_async_remote_copy(
                send.at[pl.ds(peer.start + 3, 1)],
                recv.at[pl.ds(3, 1), place.slot],
                fwd_send, fwd_recv.at[2], device_id=peer.device, device_id_type=MESH,
            ).start()

        for_peers(place, send_fwd, send_extra if k == 2 else None)

    def keep_own(count):
        copy = pltpu.make_async_copy(send.at[pl.ds(place.start, count)], recv.at[pl.ds(0, count), place.slot], own_sem)
        copy.start()
        copy.wait()

    by_turn(place, keep_own)

    finish(3)
    finish(4)
    finish(5)
    real, imag = row_buf[0], row_buf[1]
    positions = lax.broadcasted_iota(jnp.int32, (COLS, LINES), 0)

    def to_lines(f):
        chosen = (positions == line_buf[pl.ds(f, 1), :]).astype(F32).astype(BF16)
        pick = (((0,), (0,)), ((), ()))
        line_real = lax.dot_general(chosen, real, pick, preferred_element_type=F32)
        line_imag = lax.dot_general(chosen, imag, pick, preferred_element_type=F32)
        table = jnp.concatenate([line_real, line_imag], axis=0)
        turned = jnp.concatenate([-line_imag, line_real], axis=0)
        back_table[...] = jnp.concatenate([table.T, turned.T], axis=0).astype(BF16)
        table = table.astype(BF16)
        x_re, x_im = planes[f, 0], planes[f, 1]

        @pl.loop(0, COILS, unroll=2)
        def _(c):
            s_re, s_im = coil_planes[c, 0], coil_planes[c, 1]
            c_re = (s_re * x_re - s_im * x_im).astype(BF16)
            c_im = (s_re * x_im + s_im * x_re).astype(BF16)
            first, second = dot(table, c_re), dot(table, c_im)
            spectra[c, 0:LINES] = first[:LINES] - second[LINES:]
            spectra[c, LINES:] = first[LINES:] + second[:LINES]

    def to_residual(f):
        @pl.loop(0, COILS, unroll=2)
        def _(c):
            rows = spectra[c].astype(BF16)
            first, second = dot(rows, real), dot(rows, imag)
            res_re = first[:LINES] - second[LINES:] - lines_planes[f, c, 0]
            res_im = first[LINES:] + second[:LINES] - lines_planes[f, c, 1]
            residual = jnp.concatenate([res_re, res_im], axis=0).astype(BF16)
            first, second = dot(residual, real), dot(residual, imag)
            moved[c, 0:LINES] = first[:LINES] + second[LINES:]
            moved[c, LINES:] = first[LINES:] - second[:LINES]

    def to_image(f):
        total[...] = jnp.zeros_like(total)

        @pl.loop(0, COILS, unroll=2)
        def _(c):
            full = dot(back_table[...], moved[c].astype(BF16))
            s_re, s_im = coil_planes[c, 0], coil_planes[c, 1]
            b_re, b_im = full[:ROWS], full[ROWS:]
            total[0] += s_re * b_re + s_im * b_im
            total[1] += s_re * b_im - s_im * b_re

        for i in range(2):
            result[f, i] = 0.75 * planes[f, i] - 0.5 * total[i] + noise_planes[f, i]

    spot = (lax.broadcasted_iota(jnp.int32, (FRAMES, FRAMES), 0) == lax.broadcasted_iota(jnp.int32, (FRAMES, FRAMES), 1))
    column = -0.5 * jnp.sum(jnp.where(spot, weight_buf[...], 0.0), axis=1, keepdims=True)

    def up_copy(k, count):
        return pltpu.make_async_remote_copy(
            recv.at[pl.ds(k, count), pl.ds(HALF, HALF)], below.at[pl.ds(k, count)],
            z_send.at[k, 0], z_recv.at[k, 0], device_id=(place.frame, place.space + 2), device_id_type=MESH,
        )

    def down_copy(k, count):
        return pltpu.make_async_remote_copy(
            recv.at[pl.ds(k, count), pl.ds(0, HALF)], above.at[pl.ds(k, count)],
            z_send.at[k, 1], z_recv.at[k, 1], device_id=(place.frame, place.space - 2), device_id_type=MESH,
        )

    rows_in, rows_out = recv.reshape(4 * 4 * PEERS, MAIN), back.reshape(4 * 4 * PEERS, MAIN)
    rows_below, rows_above = below.reshape(4 * 4 * HALF, MAIN), above.reshape(4 * 4 * HALF, MAIN)

    def span(first, g):
        return pl.ds(4 * (PEERS * g + first), 4 * HALF)

    def arrive(k, count):
        wait_bytes(recv.at[pl.ds(k, count), pl.ds(0, PEERS - 1)], fwd_recv.at[k])

        @pl.when(place.z < 7)
        def _():
            up_copy(k, count).start()

        @pl.when(place.z > 0)
        def _():
            down_copy(k, count).start()

        blocks = [(first, g) for first in (0, HALF) for g in range(k, k + count)]
        stack = jnp.concatenate([rows_in[span(first, g), :] for first, g in blocks], axis=1)
        spectrum = exact_dot(time_buf[0], stack)
        s_re, s_im = spectrum[:FRAMES], spectrum[FRAMES:]
        scale = column * lax.rsqrt(s_re * s_re + s_im * s_im + SOFTNESS)
        shrunk = jnp.concatenate([s_re * scale, s_im * scale], axis=0)
        gradient = exact_dot(time_buf[1], shrunk)
        for n, (first, g) in enumerate(blocks):
            beside = rows_in[span(HALF - first, g), :]
            rows_out[span(first, g), :] = gradient[:, n * MAIN : (n + 1) * MAIN] + 0.125 * beside

    def leave(k, count):
        @pl.when(place.z > 0)
        def _():
            up_copy(k, count).wait_recv()
            for g in range(k, k + count):
                rows_out[span(0, g), :] += 0.125 * rows_below[pl.ds(4 * HALF * g, 4 * HALF), :]

        @pl.when(place.z < 7)
        def _():
            down_copy(k, count).wait_recv()
            for g in range(k, k + count):
                rows_out[span(HALF, g), :] += 0.125 * rows_above[pl.ds(4 * HALF * g, 4 * HALF), :]

        def send_back(peer):
            pltpu.make_async_remote_copy(
                back.at[pl.ds(k, count), peer.slot],
                ret.at[pl.ds(place.start + k, count)],
                ret_send, ret_recv, device_id=peer.device, device_id_type=MESH,
            ).start()

        for_peers(place, send_back)

    to_lines(0)
    arrive(0, 1)
    to_residual(0)
    arrive(1, 1)
    leave(0, 1)
    by_turn(place, lambda count: arrive(2, count - 2))
    leave(1, 1)
    to_image(0)
    by_turn(place, lambda count: leave(2, count - 2))
    to_lines(1)
    to_residual(1)
    to_image(1)
    keep = pltpu.make_async_copy(result, known, load_sem.at[0])
    keep.start()

    def settle(count):
        copy = pltpu.make_async_copy(back.at[pl.ds(0, count), place.slot], ret.at[pl.ds(place.start, count)], own_sem)
        copy.start()
        copy.wait()
        wait_bytes(ret.at[pl.ds(0, GROUPS - count)], ret_recv)

    by_turn(place, settle)

    def drain(count):
        wait_bytes(send.at[pl.ds(0, GROUPS - count)], fwd_send)
        wait_bytes(recv.at[pl.ds(0, count), pl.ds(0, PEERS - 1)], ret_send)

        for k in range(3):
            groups = count - 2 if k == 2 else 1

            @pl.when(place.z < 7)
            def _():
                up_copy(k, groups).wait_send()

            @pl.when(place.z > 0)
            def _():
                down_copy(k, groups).wait_send()

    by_turn(place, drain)
    keep.wait()


def assemble(ret, known, out):
    for i in range(2):
        out[0, 0, :, i, 0:MAIN] = known[0, i, :, 0:MAIN] + ret[pl.ds(0, ROWS), 0, i, :]
        tails = ret[pl.ds(ROWS, 40), 0, i, :]
        tails = jnp.concatenate([tails[:, 32 * b : 32 * b + 32] for b in range(4)], axis=0)
        out[0, 0, :, i, MAIN:COLS] = known[0, i, :, MAIN:COLS] + tails


def on_device(image, maps, measured, lines, weights, noise):
    dma = pltpu.SemaphoreType.DMA
    anywhere = pl.BlockSpec(memory_space=pl.ANY)
    ret, known = pl.pallas_call(
        kernel,
        name="langevin_step",
        out_shape=(jax.ShapeDtypeStruct((GROUPS, 2, 2, MAIN), F32), jax.ShapeDtypeStruct((2, 2, ROWS, COLS), F32)),
        in_specs=[anywhere] * 8,
        out_specs=(anywhere, anywhere),
        scratch_shapes=[
            pltpu.VMEM((GROUPS, 2, 2, MAIN), F32),
            pltpu.VMEM((4, PEERS, 2, 2, MAIN), F32),
            pltpu.VMEM((4, PEERS, 2, 2, MAIN), F32),
            pltpu.VMEM((4, HALF, 2, 2, MAIN), F32),
            pltpu.VMEM((4, HALF, 2, 2, MAIN), F32),
            pltpu.VMEM((2, 2, ROWS, COLS), F32),
            pltpu.VMEM((2, 2, ROWS, COLS), F32),
            pltpu.VMEM((COILS, ROWS, 2, COLS), BF16),
            pltpu.VMEM((COILS, 2, ROWS, COLS), F32),
            pltpu.VMEM((2, COILS, 2, LINES, COLS), F32),
            pltpu.VMEM((2, LINES), jnp.int32),
            pltpu.VMEM((1, FRAMES), F32),
            pltpu.VMEM((2, COLS, COLS), BF16),
            pltpu.VMEM((2, 2 * FRAMES, 2 * FRAMES), F32),
            pltpu.VMEM((2 * ROWS, 2 * LINES), BF16),
            pltpu.VMEM((COILS, 2 * LINES, COLS), F32),
            pltpu.VMEM((COILS, 2 * LINES, COLS), F32),
            pltpu.VMEM((2, ROWS, COLS), F32),
            pltpu.VMEM((2, 2, ROWS, COLS), F32),
            dma((6,)), dma, dma, dma((3,)), dma, dma, dma((3, 2)), dma((3, 2)),
        ],
        compiler_params=pltpu.CompilerParams(collective_id=0, has_side_effects=True, vmem_limit_bytes=60 << 20),
        cost_estimate=pl.CostEstimate(flops=2_000_000_000, bytes_accessed=6_000_000, transcendentals=60_000),
    )(image, maps, measured, lines, weights.reshape(1, FRAMES), noise, jnp.asarray(row_tables()), jnp.asarray(time_tables()))
    return pl.pallas_call(
        assemble,
        name="assemble",
        out_shape=jax.ShapeDtypeStruct(image.shape, F32),
        grid=(2,),
        in_specs=[
            pl.BlockSpec((GROUPS, 1, 2, MAIN), lambda f: (0, f, 0, 0)),
            pl.BlockSpec((1, 2, ROWS, COLS), lambda f: (f, 0, 0, 0)),
        ],
        out_specs=pl.BlockSpec((1, 1, ROWS, 2, COLS), lambda f: (f, 0, 0, 0, 0)),
        compiler_params=pltpu.CompilerParams(vmem_limit_bytes=60 << 20),
    )(ret, known)


def solution(mesh):
    return jax.shard_map(
        on_device,
        mesh=mesh,
        in_specs=(
            P("frame", "space", None, None, None),
            P("space", None, None, None, None),
            P("frame", "space", None, None, None, None),
            P("frame", None),
            P(),
            P("frame", "space", None, None, None),
        ),
        out_specs=P("frame", "space", None, None, None),
        check_vma=False,
    )
```

```python
import math

import jax
import jax.numpy as jnp
import ml_dtypes
import numpy as np
from jax import lax
from jax.experimental import pallas as pl
from jax.experimental.pallas import tpu as pltpu
from jax.sharding import PartitionSpec as P

MESH = pl.DeviceIdType.MESH
F32, BF16 = jnp.float32, jnp.bfloat16
ROWS = COLS = 160
COILS, LINES, FRAMES = 8, 40, 64
SOFTNESS = 0.01
MAIN = 128
GROUPS = 200
PEERS = 64
HALF = 32


def dft(count):
    index = np.arange(count)
    angles = 2.0 * math.pi / count * (index[:, None] * index[None, :] % count)
    return np.cos(angles) / math.sqrt(count), -np.sin(angles) / math.sqrt(count)


def row_tables():
    real, imag = dft(COLS)
    return np.stack([real, imag]).astype(np.float32).astype(ml_dtypes.bfloat16)


def time_tables():
    real, imag = dft(FRAMES)
    upper = np.stack([real, -imag], axis=-1).reshape(FRAMES, 2 * FRAMES)
    lower = np.stack([imag, real], axis=-1).reshape(FRAMES, 2 * FRAMES)
    forward = np.concatenate([upper, lower], axis=0)
    return np.stack([forward, forward.T]).astype(np.float32)


def dot(a, b):
    return jnp.dot(a, b, preferred_element_type=F32)


def exact_dot(a, b):
    return jnp.dot(a, b, precision=lax.Precision.HIGHEST, preferred_element_type=F32)


class Place:
    def __init__(self):
        self.frame, self.space = lax.axis_index("frame"), lax.axis_index("space")
        self.base = self.space // 2 * 2
        self.z = self.space // 2
        self.y = self.frame // 8 * 2 + self.space % 2
        x, core = self.frame // 2 % 4, self.frame % 2
        self.xs = [(x + dx) % 4 for dx in FAR_X]
        self.cores = [1 - core, core]
        self.turn = (x + self.y) % 4 * 2 + core
        self.slot = self.space % 2 * HALF + self.frame
        self.start = 25 * self.y + 3 * self.turn


class Peer:
    def __init__(self, frame, space, slot, start):
        self.device, self.slot, self.start = (frame, space), slot, start


FAR_X = (2, 1, 3, 0)


def row_of(place, y):
    frame, space, slot, start = y // 2 * 8, place.base + y % 2, y % 2 * HALF + y // 2 * 8, 25 * y
    peers = []
    for x in place.xs:
        first = start + 6 * ((x + y) % 4)
        for core in place.cores:
            at = 2 * x + core
            peers.append(Peer(frame + at, space, slot + at, first + 3 * core))
    extra = (7 - y) % 4 * 2 + 1
    return peers, Peer(frame + extra, space, slot + extra, start + 21)


def distance(a):
    return (1 - a % 2) * (4 + a // 2) + a % 2 * (4 - (a + 1) // 2)


def for_peers(place, body, each_row=None):
    @pl.loop(0, 7)
    def _(a):
        peers, extra = row_of(place, (place.y + distance(a)) % 8)
        for peer in peers:
            body(peer, a)
        if each_row is not None:
            each_row(extra, a)

    peers, extra = row_of(place, place.y)
    for peer in peers[:-1]:
        body(peer, 7)
    if each_row is not None:

        @pl.when(place.turn != 7)
        def _():
            each_row(extra, 7)


def by_turn(place, body):
    @pl.when(place.turn != 7)
    def _():
        body(3)

    @pl.when(place.turn == 7)
    def _():
        body(4)


def wait_bytes(ref, semaphore):
    pltpu.make_async_copy(ref, ref, semaphore).wait()


def kernel(
    image, maps, measured, lines, weights, noise, row_table, time_table,
    ret, known,
    send, recv, back, below, above, planes, noise_planes, raw_maps, coil_planes, lines_planes,
    line_buf, weight_buf, row_buf, time_buf, back_table, spectra, moved, total, result,
    load_sem, own_sem, fwd_send, fwd_recv, ret_send, ret_recv, z_send, z_recv,
):
    place = Place()
    loads = [
        [pltpu.make_async_copy(image.at[f, 0, :, i, :], planes.at[f, i], load_sem.at[0]) for f in range(2) for i in range(2)],
        [pltpu.make_async_copy(image.at[f, 0, :, :, pl.ds(0, MAIN)], send.at[pl.ds(0, ROWS), f], load_sem.at[1]) for f in range(2)],
        [pltpu.make_async_copy(maps.at[0], raw_maps, load_sem.at[2])],
        [
            pltpu.make_async_copy(row_table, row_buf, load_sem.at[3]),
            pltpu.make_async_copy(lines, line_buf, load_sem.at[3]),
            pltpu.make_async_copy(weights, weight_buf, load_sem.at[3]),
            pltpu.make_async_copy(time_table, time_buf, load_sem.at[3]),
        ],
        [pltpu.make_async_copy(measured.at[f, 0, :, :, i, :], lines_planes.at[f, :, i], load_sem.at[4]) for f in range(2) for i in range(2)],
        [pltpu.make_async_copy(noise.at[f, 0, :, i, :], noise_planes.at[f, i], load_sem.at[5]) for f in range(2) for i in range(2)],
    ]
    for copy in loads[1] + loads[0]:
        copy.start()

    def finish(which):
        for copy in loads[which]:
            copy.wait()

    barrier = pltpu.get_barrier_semaphore()

    def greet(peer, a):
        pl.semaphore_signal(barrier, inc=1, device_id=peer.device, device_id_type=MESH)

    for_peers(place, greet)
    for group in loads[2:]:
        for copy in group:
            copy.start()

    @pl.when(place.z < 7)
    def _():
        pl.semaphore_signal(barrier, inc=1, device_id=(place.frame, place.space + 2), device_id_type=MESH)

    @pl.when(place.z > 0)
    def _():
        pl.semaphore_signal(barrier, inc=1, device_id=(place.frame, place.space - 2), device_id_type=MESH)

    finish(0)
    finish(1)
    for f in range(2):
        for i in range(2):
            tails = [planes[f, i, 40 * b : 40 * b + 40, MAIN:COLS] for b in range(4)]
            send[pl.ds(ROWS, 40), f, i, :] = jnp.concatenate(tails, axis=1)

    finish(2)

    @pl.loop(0, COILS)
    def _(c):
        for i in range(2):
            coil_planes[c, i] = raw_maps[c, :, i, :].astype(F32)

    @pl.when((place.z == 0) | (place.z == 7))
    def _():
        pl.semaphore_wait(barrier, PEERS)

    @pl.when((place.z != 0) & (place.z != 7))
    def _():
        pl.semaphore_wait(barrier, PEERS + 1)

    for k in range(3):

        def send_fwd(peer, a):
            pltpu.make_async_remote_copy(
                send.at[pl.ds(peer.start + k, 1)],
                recv.at[pl.ds(k, 1), place.slot],
                fwd_send, fwd_recv.at[k, a], device_id=peer.device, device_id_type=MESH,
            ).start()

        def send_extra(peer, a):
            pltpu.make_async_remote_copy(
                send.at[pl.ds(peer.start + 3, 1)],
                recv.at[pl.ds(3, 1), place.slot],
                fwd_send, fwd_recv.at[2, a], device_id=peer.device, device_id_type=MESH,
            ).start()

        for_peers(place, send_fwd, send_extra if k == 2 else None)

    def keep_own(count):
        copy = pltpu.make_async_copy(send.at[pl.ds(place.start, count)], recv.at[pl.ds(0, count), place.slot], own_sem)
        copy.start()
        copy.wait()

    by_turn(place, keep_own)

    finish(3)
    finish(4)
    finish(5)
    real, imag = row_buf[0], row_buf[1]
    positions = lax.broadcasted_iota(jnp.int32, (COLS, LINES), 0)

    def to_lines(f):
        chosen = (positions == line_buf[pl.ds(f, 1), :]).astype(F32).astype(BF16)
        pick = (((0,), (0,)), ((), ()))
        line_real = lax.dot_general(chosen, real, pick, preferred_element_type=F32)
        line_imag = lax.dot_general(chosen, imag, pick, preferred_element_type=F32)
        table = jnp.concatenate([line_real, line_imag], axis=0)
        turned = jnp.concatenate([-line_imag, line_real], axis=0)
        back_table[...] = jnp.concatenate([table.T, turned.T], axis=0).astype(BF16)
        table = table.astype(BF16)
        x_re, x_im = planes[f, 0], planes[f, 1]

        @pl.loop(0, COILS, unroll=2)
        def _(c):
            s_re, s_im = coil_planes[c, 0], coil_planes[c, 1]
            c_re = (s_re * x_re - s_im * x_im).astype(BF16)
            c_im = (s_re * x_im + s_im * x_re).astype(BF16)
            first, second = dot(table, c_re), dot(table, c_im)
            spectra[c, 0:LINES] = first[:LINES] - second[LINES:]
            spectra[c, LINES:] = first[LINES:] + second[:LINES]

    def to_residual(f):
        @pl.loop(0, COILS, unroll=2)
        def _(c):
            rows = spectra[c].astype(BF16)
            first, second = dot(rows, real), dot(rows, imag)
            res_re = first[:LINES] - second[LINES:] - lines_planes[f, c, 0]
            res_im = first[LINES:] + second[:LINES] - lines_planes[f, c, 1]
            residual = jnp.concatenate([res_re, res_im], axis=0).astype(BF16)
            first, second = dot(residual, real), dot(residual, imag)
            moved[c, 0:LINES] = first[:LINES] + second[LINES:]
            moved[c, LINES:] = first[LINES:] - second[:LINES]

    def to_image(f):
        total[...] = jnp.zeros_like(total)

        @pl.loop(0, COILS, unroll=2)
        def _(c):
            full = dot(back_table[...], moved[c].astype(BF16))
            s_re, s_im = coil_planes[c, 0], coil_planes[c, 1]
            b_re, b_im = full[:ROWS], full[ROWS:]
            total[0] += s_re * b_re + s_im * b_im
            total[1] += s_re * b_im - s_im * b_re

        for i in range(2):
            result[f, i] = 0.75 * planes[f, i] - 0.5 * total[i] + noise_planes[f, i]

    spot = (lax.broadcasted_iota(jnp.int32, (FRAMES, FRAMES), 0) == lax.broadcasted_iota(jnp.int32, (FRAMES, FRAMES), 1))
    column = -0.5 * jnp.sum(jnp.where(spot, weight_buf[...], 0.0), axis=1, keepdims=True)

    def up_copy(k, count, slot=0, width=HALF):
        return pltpu.make_async_remote_copy(
            recv.at[pl.ds(k, count), pl.ds(HALF + slot, width)], below.at[pl.ds(k, count), pl.ds(slot, width)],
            z_send.at[k, 0], z_recv.at[k, 0], device_id=(place.frame, place.space + 2), device_id_type=MESH,
        )

    def down_copy(k, count, slot=0, width=HALF):
        return pltpu.make_async_remote_copy(
            recv.at[pl.ds(k, count), pl.ds(slot, width)], above.at[pl.ds(k, count), pl.ds(slot, width)],
            z_send.at[k, 1], z_recv.at[k, 1], device_id=(place.frame, place.space - 2), device_id_type=MESH,
        )

    rows_in, rows_out = recv.reshape(4 * 4 * PEERS, MAIN), back.reshape(4 * 4 * PEERS, MAIN)
    rows_below, rows_above = below.reshape(4 * 4 * HALF, MAIN), above.reshape(4 * 4 * HALF, MAIN)

    def span(first, g):
        return pl.ds(4 * (PEERS * g + first), 4 * HALF)

    def arrive(k, count):
        def hand_on(y):
            @pl.when((y % 2 == 1) & (place.z < 7))
            def _():
                up_copy(k, count, y // 2 * 8, 8).start()

            @pl.when((y % 2 == 0) & (place.z > 0))
            def _():
                down_copy(k, count, y // 2 * 8, 8).start()

        @pl.loop(0, 7)
        def _(a):
            wait_bytes(recv.at[pl.ds(k, count), pl.ds(0, 8)], fwd_recv.at[k, a])
            hand_on((place.y + 8 - distance(a)) % 8)

        wait_bytes(recv.at[pl.ds(k, count), pl.ds(0, 7)], fwd_recv.at[k, 7])
        hand_on(place.y)

        blocks = [(first, g) for first in (0, HALF) for g in range(k, k + count)]
        stack = jnp.concatenate([rows_in[span(first, g), :] for first, g in blocks], axis=1)
        spectrum = exact_dot(time_buf[0], stack)
        s_re, s_im = spectrum[:FRAMES], spectrum[FRAMES:]
        scale = column * lax.rsqrt(s_re * s_re + s_im * s_im + SOFTNESS)
        shrunk = jnp.concatenate([s_re * scale, s_im * scale], axis=0)
        gradient = exact_dot(time_buf[1], shrunk)
        for n, (first, g) in enumerate(blocks):
            beside = rows_in[span(HALF - first, g), :]
            rows_out[span(first, g), :] = gradient[:, n * MAIN : (n + 1) * MAIN] + 0.125 * beside

    def leave(k, count):
        @pl.when(place.z > 0)
        def _():
            up_copy(k, count).wait_recv()
            for g in range(k, k + count):
                rows_out[span(0, g), :] += 0.125 * rows_below[pl.ds(4 * HALF * g, 4 * HALF), :]

        @pl.when(place.z < 7)
        def _():
            down_copy(k, count).wait_recv()
            for g in range(k, k + count):
                rows_out[span(HALF, g), :] += 0.125 * rows_above[pl.ds(4 * HALF * g, 4 * HALF), :]

        def send_back(peer, a):
            pltpu.make_async_remote_copy(
                back.at[pl.ds(k, count), peer.slot],
                ret.at[pl.ds(place.start + k, count)],
                ret_send, ret_recv, device_id=peer.device, device_id_type=MESH,
            ).start()

        for_peers(place, send_back)

    to_lines(0)
    arrive(0, 1)
    to_residual(0)
    leave(0, 1)
    arrive(1, 1)
    by_turn(place, lambda count: arrive(2, count - 2))
    leave(1, 1)
    to_image(0)
    by_turn(place, lambda count: leave(2, count - 2))
    to_lines(1)
    to_residual(1)
    to_image(1)
    keep = pltpu.make_async_copy(result, known, load_sem.at[0])
    keep.start()

    def settle(count):
        copy = pltpu.make_async_copy(back.at[pl.ds(0, count), place.slot], ret.at[pl.ds(place.start, count)], own_sem)
        copy.start()
        copy.wait()
        wait_bytes(ret.at[pl.ds(0, GROUPS - count)], ret_recv)

    by_turn(place, settle)

    def drain(count):
        wait_bytes(send.at[pl.ds(0, GROUPS - count)], fwd_send)
        wait_bytes(recv.at[pl.ds(0, count), pl.ds(0, PEERS - 1)], ret_send)

        for k in range(3):
            groups = count - 2 if k == 2 else 1

            @pl.when(place.z < 7)
            def _():
                up_copy(k, groups).wait_send()

            @pl.when(place.z > 0)
            def _():
                down_copy(k, groups).wait_send()

    by_turn(place, drain)
    keep.wait()


def assemble(ret, known, out):
    for i in range(2):
        out[0, 0, :, i, 0:MAIN] = known[0, i, :, 0:MAIN] + ret[pl.ds(0, ROWS), 0, i, :]
        tails = ret[pl.ds(ROWS, 40), 0, i, :]
        tails = jnp.concatenate([tails[:, 32 * b : 32 * b + 32] for b in range(4)], axis=0)
        out[0, 0, :, i, MAIN:COLS] = known[0, i, :, MAIN:COLS] + tails


def on_device(image, maps, measured, lines, weights, noise):
    dma = pltpu.SemaphoreType.DMA
    anywhere = pl.BlockSpec(memory_space=pl.ANY)
    ret, known = pl.pallas_call(
        kernel,
        name="langevin_step",
        out_shape=(jax.ShapeDtypeStruct((GROUPS, 2, 2, MAIN), F32), jax.ShapeDtypeStruct((2, 2, ROWS, COLS), F32)),
        in_specs=[anywhere] * 8,
        out_specs=(anywhere, anywhere),
        scratch_shapes=[
            pltpu.VMEM((GROUPS, 2, 2, MAIN), F32),
            pltpu.VMEM((4, PEERS, 2, 2, MAIN), F32),
            pltpu.VMEM((4, PEERS, 2, 2, MAIN), F32),
            pltpu.VMEM((4, HALF, 2, 2, MAIN), F32),
            pltpu.VMEM((4, HALF, 2, 2, MAIN), F32),
            pltpu.VMEM((2, 2, ROWS, COLS), F32),
            pltpu.VMEM((2, 2, ROWS, COLS), F32),
            pltpu.VMEM((COILS, ROWS, 2, COLS), BF16),
            pltpu.VMEM((COILS, 2, ROWS, COLS), F32),
            pltpu.VMEM((2, COILS, 2, LINES, COLS), F32),
            pltpu.VMEM((2, LINES), jnp.int32),
            pltpu.VMEM((1, FRAMES), F32),
            pltpu.VMEM((2, COLS, COLS), BF16),
            pltpu.VMEM((2, 2 * FRAMES, 2 * FRAMES), F32),
            pltpu.VMEM((2 * ROWS, 2 * LINES), BF16),
            pltpu.VMEM((COILS, 2 * LINES, COLS), F32),
            pltpu.VMEM((COILS, 2 * LINES, COLS), F32),
            pltpu.VMEM((2, ROWS, COLS), F32),
            pltpu.VMEM((2, 2, ROWS, COLS), F32),
            dma((6,)), dma, dma, dma((3, 8)), dma, dma, dma((3, 2)), dma((3, 2)),
        ],
        compiler_params=pltpu.CompilerParams(collective_id=0, has_side_effects=True, vmem_limit_bytes=60 << 20),
        cost_estimate=pl.CostEstimate(flops=2_000_000_000, bytes_accessed=6_000_000, transcendentals=60_000),
    )(image, maps, measured, lines, weights.reshape(1, FRAMES), noise, jnp.asarray(row_tables()), jnp.asarray(time_tables()))
    return pl.pallas_call(
        assemble,
        name="assemble",
        out_shape=jax.ShapeDtypeStruct(image.shape, F32),
        grid=(2,),
        in_specs=[
            pl.BlockSpec((GROUPS, 1, 2, MAIN), lambda f: (0, f, 0, 0)),
            pl.BlockSpec((1, 2, ROWS, COLS), lambda f: (f, 0, 0, 0)),
        ],
        out_specs=pl.BlockSpec((1, 1, ROWS, 2, COLS), lambda f: (f, 0, 0, 0, 0)),
        compiler_params=pltpu.CompilerParams(vmem_limit_bytes=60 << 20),
    )(ret, known)


def solution(mesh):
    return jax.shard_map(
        on_device,
        mesh=mesh,
        in_specs=(
            P("frame", "space", None, None, None),
            P("space", None, None, None, None),
            P("frame", "space", None, None, None, None),
            P("frame", None),
            P(),
            P("frame", "space", None, None, None),
        ),
        out_specs=P("frame", "space", None, None, None),
        check_vma=False,
    )
```
